512 devices in a mesh: dp: 64 (over y, z_lo, core), tensor: 8 (over x, z_hi).
Axes of the slice: x: 4, y: 8, z: 8 (z_hi: 2, z_lo: 4; z = z_hi * 4 + z_lo), core: 2. Of those that a mesh axis runs over, the one named last changes fastest.
Arguments:
- cache: bfloat16 [256, 1024, 576], P(None, ('dp', 'tensor')), may hold values from -6 to 6
- queries: bfloat16 [256, 3, 128, 576], P('dp', None, 'tensor'), may hold values from -36 to 36
- new_latent: bfloat16 [256, 3, 576], P('dp'), may hold values from -8 to 8
- lengths: int32 [256], replicated, may hold values from 256 to 1024, as said below
- assignment: int32 [256], replicated, may hold values from 0 to 255, each once
- value_weight: bfloat16 [128, 512, 128], P('tensor'), may hold values from -0.25 to 0.25
- output_weight: bfloat16 [16384, 7168], P('tensor', 'dp'), may hold values from -0.046875 to 0.046875
Outputs:
- layer_out: bfloat16 [256, 3, 7168], P(None, None, ('dp', 'tensor'))
The draws below stay inside these ranges and needn't reach their ends.
Inputs may be any that keep to these rules, and one draw needn't show every extreme that they name: `lengths`: some request has exactly 1024 prefilled positions and some exactly 256. `assignment`: each request is held by exactly one slot.
All inputs are finite; a program needn't handle non-finite values.
Results may differ from the reference program's by a relative error of at most 0.015.
Values may be sent and summed in bfloat16 or wider, within the bound.
No kernel may reach another device: no remote copies, remote signals or barrier semaphores. Data moves between devices by JAX's collectives and lax.ppermute only.
A program may use at most 64 MiB of HBM per device.

```python
import jax
import jax.numpy as jnp
from jax import lax

C_LAT = 512
ROPE = 64
HEADS = 128
VHEAD = 128
D = 7168
STEPS = 3
R = 256
SEQ = 1024


def latent_pair(key):
    width = C_LAT + ROPE
    base = jax.random.normal(jax.random.fold_in(key, 101), (R, STEPS, width), jnp.float32)
    return jnp.clip(base, -6.0, 6.0)


def draw_new_latent(key, part):
    base = latent_pair(key)
    return base.astype(jnp.bfloat16)


def draw_queries(key, part):
    key = jax.random.fold_in(key, 2)
    fresh = jnp.clip(jax.random.normal(key, (R, STEPS, HEADS, C_LAT + ROPE), jnp.float32), -6.0, 6.0) * 1.5
    return fresh.astype(jnp.bfloat16)


def draw_lengths(key, part):
    key = jax.random.fold_in(key, 4)
    counts = jax.random.randint(jax.random.fold_in(key, 1), (R,), SEQ // 4, SEQ + 1)
    first = jax.random.randint(jax.random.fold_in(key, 2), (), 0, R)
    second = (first + 1 + jax.random.randint(jax.random.fold_in(key, 3), (), 0, R - 1)) % R
    counts = counts.at[first].set(SEQ).at[second].set(SEQ // 4)
    return counts.astype(jnp.int32)


def block_scale(rng, extent, shards, low, top_value):
    gain = 1.0
    for position, shards_of in shards:
        heights = jax.random.uniform(jax.random.fold_in(jax.random.fold_in(rng, 6), position), (shards_of,), jnp.float32, low / len(shards), top_value / len(shards))
        gain = gain * jnp.repeat(jnp.exp(heights), extent[position] // shards_of).reshape((-1,) + (1,) * (len(extent) - 1 - position))
    return gain


def noise(key, extent, scale, bound, pieces=(), dtype=jnp.bfloat16):
    loudness = block_scale(key, extent, pieces, -0.22, 0.18) if pieces else 1.0
    result = jax.random.normal(key, extent, jnp.float32) * scale * loudness
    return jnp.minimum(jnp.maximum(result, -bound), bound).astype(dtype)


def setup_inputs(seed: int = 0) -> dict:
    streams_of = jax.random.split(jax.random.key(seed), 8)
    cache = noise(streams_of[0], (R, SEQ, C_LAT + ROPE), 1.0, 6.0, ((1, 512),))
    queries = draw_queries(jax.random.fold_in(streams_of[7], 71), 0)
    new_latent = draw_new_latent(jax.random.fold_in(streams_of[7], 71), 0)
    lengths = draw_lengths(jax.random.fold_in(streams_of[7], 71), 0)
    assignment = jax.random.permutation(streams_of[4], R).astype(jnp.int32)
    value_weight = noise(streams_of[5], (HEADS, C_LAT, VHEAD), C_LAT ** -0.5, 0.25, ((0, 8),))
    output_weight = noise(streams_of[6], (HEADS * VHEAD, D), (HEADS * VHEAD) ** -0.5, 0.046875, ((0, 8), (1, 64)))
    return {"cache": cache, "queries": queries, "new_latent": new_latent, "lengths": lengths, "assignment": assignment, "value_weight": value_weight, "output_weight": output_weight}


score_scale = 192.0 ** -0.5
lowest = -1.0e30


def reference(cache, queries, new_latent, lengths, assignment, value_weight, output_weight):
    slot_lengths = jnp.take(lengths, assignment)
    places = jnp.arange(SEQ + STEPS)
    step_index = jnp.arange(STEPS)

    def one_slot(items):
        slot_query, slot_new, request, limit = items
        prefilled = lax.dynamic_index_in_dim(cache, request.astype(jnp.int32), 0, keepdims=False)
        keys = jnp.concatenate([prefilled, slot_new], axis=0)
        scores = jnp.einsum('shc,kc->shk', slot_query.astype(jnp.float32), keys.astype(jnp.float32)) * score_scale
        live = jnp.where(places[None, :] < SEQ, places[None, :] < limit, (places[None, :] - SEQ) <= step_index[:, None])
        live = live[:, None, :]
        masked = jnp.where(live, scores, lowest)
        top = jnp.max(masked, axis=-1, keepdims=True)
        raised = jnp.where(live, jnp.exp(masked - top), 0.0)
        total = jnp.sum(raised, axis=-1, keepdims=True)
        weight = raised.astype(jnp.bfloat16)
        summed = jnp.einsum('shk,kc->shc', weight.astype(jnp.float32), keys[:, :C_LAT].astype(jnp.float32))
        latent_out = (summed / total).astype(jnp.bfloat16)
        head_out = jnp.einsum('shc,hcv->shv', latent_out.astype(jnp.float32), value_weight.astype(jnp.float32))
        return head_out.astype(jnp.bfloat16)

    heads_out = lax.map(one_slot, (queries, new_latent, assignment, slot_lengths))
    flat = heads_out.reshape(R * STEPS, HEADS * VHEAD)
    layer_out = jnp.dot(flat, output_weight, preferred_element_type=jnp.float32).astype(jnp.bfloat16)
    return layer_out.reshape(R, STEPS, D)
```

```python
import jax
import jax.numpy as jnp
from jax import lax
from jax.sharding import Mesh, PartitionSpec as P

score_scale = 192.0 ** (-0.5)
lowest = -1e30

DP = ("y", "za", "zb", "core")
TENSOR = ("x", "zh")
SIZES = (("y", 8), ("za", 2), ("zb", 2), ("core", 2), ("x", 4), ("zh", 2))


def swap(array, axis):
    return lax.ppermute(array, axis, [(0, 1), (1, 0)])


def in_order(own, other, axis, dim):
    first = lax.axis_index(axis) == 0
    return jnp.concatenate([jnp.where(first, own, other), jnp.where(first, other, own)], axis=dim)


def split_three(value):
    high = lax.reduce_precision(value, 8, 7)
    rest = value - high
    middle = lax.reduce_precision(rest, 8, 7)
    low = rest - middle
    return [part.astype(jnp.bfloat16) for part in (high, middle, low)]


def on_device(cache, queries, new_latent, lengths, assignment, value_weight, output_weight):
    slots, steps, heads, depth = queries.shape
    requests = cache.shape[0]
    width = value_weight.shape[1]
    vhead = value_weight.shape[2]
    x_count, zh_count = lax.axis_size("x"), lax.axis_size("zh")
    groups = x_count * zh_count
    x_place, zh_place = lax.axis_index("x"), lax.axis_index("zh")
    dp_place = lax.axis_index(DP)

    weight = output_weight.T
    weight = in_order(weight, swap(weight, "zb"), "zb", 0)
    columns = output_weight.shape[1]
    other = swap(weight, "core")
    weight = in_order(
        weight.reshape(2, 1, columns, -1), other.reshape(2, 1, columns, -1), "core", 1
    ).reshape(4 * columns, -1)

    mine = lax.all_to_all(queries, "x", split_axis=0, concat_axis=0, tiled=True)
    theirs = swap(mine, "zh")
    query = jnp.concatenate([mine, theirs], axis=0).reshape(-1, depth)

    order = (assignment[:, None] == jnp.arange(requests)[None, :]).astype(jnp.bfloat16)
    ordered = jnp.einsum(
        "jr,rpc->jpc", order, cache, preferred_element_type=jnp.float32
    ).astype(jnp.bfloat16)
    keys = lax.all_to_all(ordered, DP + ("x",), split_axis=0, concat_axis=0, tiled=True)
    block = cache.shape[1]
    keys = keys.reshape(-1, depth)
    index = jnp.arange(keys.shape[0])
    source = index // block
    places = (source // x_count * groups + source % x_count * zh_count + zh_place) * block + index % block
    slot = dp_place * slots + x_place
    limit = lengths[assignment[slot]]

    fresh = lax.dynamic_index_in_dim(new_latent, x_place, 0, keepdims=False)
    score = jnp.einsum("qc,kc->qk", query, keys, preferred_element_type=jnp.float32) * score_scale
    score = jnp.where((places < limit)[None, :], score, lowest)
    step_of = jnp.arange(query.shape[0]) // heads % steps
    live = (jnp.arange(steps)[None, :] <= step_of[:, None]) & (zh_place == 0)
    fresh_score = jnp.einsum("qc,kc->qk", query, fresh, preferred_element_type=jnp.float32) * score_scale
    fresh_score = jnp.where(live, fresh_score, lowest)
    top = jnp.maximum(jnp.max(score, axis=1), jnp.max(fresh_score, axis=1))[:, None]
    raised = jnp.exp(score - top)
    fresh_raised = jnp.exp(fresh_score - top)
    total = jnp.sum(raised, axis=1, keepdims=True) + jnp.sum(fresh_raised, axis=1, keepdims=True)
    summed = jnp.einsum(
        "qk,kc->qc", raised.astype(jnp.bfloat16), keys[:, :width], preferred_element_type=jnp.float32
    ) + jnp.einsum(
        "qk,kc->qc", fresh_raised.astype(jnp.bfloat16), fresh[:, :width], preferred_element_type=jnp.float32
    )
    partial = (summed / total).astype(jnp.bfloat16)
    marks = jnp.concatenate(split_three(top) + split_three(total), axis=1)
    marks = jnp.pad(marks, ((0, 0), (0, 128 - marks.shape[1])))
    partial = jnp.concatenate([partial, marks], axis=1)
    rows = steps * heads
    partial = partial.reshape(2, x_count, rows, width + 128)
    first = zh_place == 0
    partial = jnp.stack(
        [jnp.where(first, partial[0], partial[1]), jnp.where(first, partial[1], partial[0])], axis=1
    ).reshape(groups, rows, width + 128)

    partial = lax.all_to_all(partial, TENSOR, split_axis=0, concat_axis=0, tiled=True)
    partial = partial.reshape(x_count, zh_count, rows, -1).astype(jnp.float32)
    value, marks = partial[..., :width], partial[..., width:]
    top = marks[..., 0:1] + marks[..., 1:2] + marks[..., 2:3]
    total = marks[..., 3:4] + marks[..., 4:5] + marks[..., 5:6]
    share = total * jnp.exp(top - jnp.max(top, axis=1, keepdims=True))
    share = share / jnp.sum(share, axis=1, keepdims=True)
    latent = jnp.sum(value * share, axis=1).astype(jnp.bfloat16)
    latent = latent.reshape(slots * steps, heads, width)
    head_out = jnp.einsum(
        "rhc,hcv->rhv", latent, value_weight, preferred_element_type=jnp.float32
    ).astype(jnp.bfloat16)

    wide = ("y", "za")
    count = lax.axis_size("y") * lax.axis_size("za")
    head_out = head_out.reshape(1, slots * steps * heads // 8, vhead * 8)
    sent = jnp.broadcast_to(head_out, (count,) + head_out.shape[1:])
    piece = lax.all_to_all(sent, wide, split_axis=0, concat_axis=0, tiled=True)
    piece = piece.reshape(count * slots * steps, heads * vhead)
    product = jnp.einsum(
        "nk,mk->nm", weight, piece, preferred_element_type=jnp.float32
    ).astype(jnp.bfloat16)
    own_columns = columns // groups
    product = product.reshape(4 * groups, own_columns, -1)
    terms = lax.all_to_all(product, ("zb", "core") + TENSOR, split_axis=0, concat_axis=0, tiled=True)
    terms = terms.reshape(4, groups, own_columns, -1)
    result = jnp.sum(terms.astype(jnp.float32), axis=1).astype(jnp.bfloat16)
    result = result.reshape(4, own_columns, count, slots, steps)
    return result.transpose(2, 0, 3, 4, 1).reshape(requests, steps, own_columns)


def solution(mesh):
    names = tuple(name for name, _ in SIZES)
    fine = Mesh(mesh.devices.reshape(tuple(size for _, size in SIZES)), names)
    return jax.shard_map(
        on_device,
        mesh=fine,
        in_specs=(
            P(None, DP + TENSOR, None),
            P(DP, None, TENSOR, None),
            P(DP, None, None),
            P(),
            P(),
            P(TENSOR, None, None),
            P(TENSOR, DP),
        ),
        out_specs=P(None, None, DP + TENSOR),
        check_vma=False,
    )
```

```python
import functools

import jax
import jax.numpy as jnp
import numpy as np
from jax import lax
from jax.experimental import pallas as pl
from jax.experimental.pallas import tpu as pltpu
from jax.sharding import Mesh, PartitionSpec as P

score_scale = 192.0 ** (-0.5)
lowest = -1e30

DP = ("yh", "yl", "za", "zb", "core")
TENSOR = ("x", "zh")
SIZES = (("yh", 4), ("yl", 2), ("za", 2), ("zb", 2), ("core", 2), ("x", 4), ("zh", 2))
WIDE = ("yh", "za", "zb")
BLOCKS = ("yl", "core")

VMEM = pl.BlockSpec(memory_space=pltpu.VMEM)
SMEM = pl.BlockSpec(memory_space=pltpu.SMEM)


def swap(array, axis):
    return lax.ppermute(array, axis, [(0, 1), (1, 0)])


def dot(a, b):
    return jnp.dot(a, b, preferred_element_type=jnp.float32)


def dot_rows(a, b):
    return lax.dot_general(a, b, (((1,), (1,)), ((), ())), preferred_element_type=jnp.float32)


def attend(steps, heads, width, place_ref, q0, q1, q2, q3, key_ref, fresh_ref, out_ref):
    x, limit = place_ref[0], place_ref[1]
    rows = steps * heads
    query = jnp.concatenate([q[...] for q in (q0, q1, q2, q3)], axis=0)
    keys = key_ref[...]
    fresh = fresh_ref[x]
    score = dot_rows(query, keys) * score_scale
    places = lax.broadcasted_iota(jnp.int32, (1, keys.shape[0]), 1)
    score = jnp.where(places < limit, score, lowest)
    fresh_score = dot_rows(query, fresh) * score_scale
    row = lax.broadcasted_iota(jnp.int32, fresh_score.shape, 0)
    column = lax.broadcasted_iota(jnp.int32, fresh_score.shape, 1)
    live = column <= (row % rows) // heads
    fresh_score = jnp.where(live, fresh_score, lowest)
    top = jnp.maximum(
        jnp.max(score, axis=1, keepdims=True), jnp.max(fresh_score, axis=1, keepdims=True)
    )
    raised = jnp.exp(score - top)
    fresh_raised = jnp.exp(fresh_score - top)
    total = jnp.sum(raised, axis=1, keepdims=True) + jnp.sum(fresh_raised, axis=1, keepdims=True)
    summed = dot(raised.astype(jnp.bfloat16), keys[:, :width]) + dot(
        fresh_raised.astype(jnp.bfloat16), fresh[:, :width]
    )
    latent = (summed / total).astype(jnp.bfloat16)
    for shift in range(4):
        out_ref[lax.rem(x + 4 - shift, 4)] = latent[shift * rows : (shift + 1) * rows]


def map_values(count, heads, latent_ref, pick_ref, value_ref, weight_ref, out_ref):
    latent = jnp.concatenate([latent_ref[slot] for slot in range(4)], axis=0)
    picked = dot(pick_ref[...], latent).astype(jnp.bfloat16)
    lines = out_ref.shape[1]
    half = heads // 2
    vhead = value_ref.shape[2]
    for h in range(half):
        value = dot(picked[h * lines : (h + 1) * lines], value_ref[h]) + dot(
            picked[(h + half) * lines : (h + half + 1) * lines], value_ref[h + half]
        )
        value = value.astype(jnp.bfloat16)
        for copy in range(count):
            out_ref[copy, :, h * vhead : (h + 1) * vhead] = value


def project(place_ref, piece_ref, order_ref, w0, w1, w2, w3, out_ref):
    yl, core = place_ref[0], place_ref[1]
    lines = dot(order_ref[...], piece_ref[...]).astype(jnp.bfloat16)
    rows, depth = lines.shape[0] // 2, lines.shape[1]
    groups = out_ref.shape[0] // 4
    columns = out_ref.shape[1]
    weight = jnp.concatenate([w[...] for w in (w0, w1, w2, w3)], axis=0)
    product = dot_rows(weight[:, :depth], lines[:rows]) + dot_rows(weight[:, depth:], lines[rows:])
    for block in range(4):
        other_y, other_core = block // 2, block % 2
        member = (1 - yl if other_y else yl) * 2 + (1 - core if other_core else core)
        for group in range(groups):
            start = (block * groups + group) * columns
            out_ref[member * groups + group] = product[start : start + columns].astype(jnp.bfloat16)


def pick_rows(slots_steps, heads):
    n = slots_steps
    pick = np.zeros((heads * 2 * n, n * heads), np.float32)
    for h in range(heads):
        for r in range(n):
            pick[h * 2 * n + (h // (heads // 2)) * n + r, r * heads + h] = 1.0
    return jnp.asarray(pick, jnp.bfloat16)


def order_rows(count, n):
    order = np.zeros((2 * count * n, 2 * count * n), np.float32)
    for half in range(2):
        for block in range(count):
            for r in range(n):
                order[(half * count + block) * n + r, (block * 2 + half) * n + r] = 1.0
    return jnp.asarray(order, jnp.bfloat16)


def on_device(cache, queries, new_latent, lengths, assignment, value_weight, output_weight):
    slots, steps, heads, depth = queries.shape
    requests, block = cache.shape[:2]
    width, vhead = value_weight.shape[1:]
    x_place, zh_count = lax.axis_index("x"), lax.axis_size("zh")
    groups = lax.axis_size("x") * zh_count
    rows = steps * heads

    order = (jnp.repeat(assignment, zh_count)[:, None] == jnp.arange(requests)[None, :]).astype(jnp.bfloat16)
    ordered = jnp.einsum(
        "jr,rpc->jpc", order, cache, preferred_element_type=jnp.float32
    ).astype(jnp.bfloat16)
    keys = lax.all_to_all(ordered, DP + TENSOR, split_axis=0, concat_axis=0, tiled=True)

    query = []
    for shift in range(4):
        both = lax.dynamic_index_in_dim(queries, lax.rem(x_place + shift, 4), 0, keepdims=False)
        both = both.reshape(rows, depth)
        if shift:
            both = lax.ppermute(both, "x", [(j, (j + shift) % 4) for j in range(4)])
        query.append(both)

    weight, keys, *query = lax.optimization_barrier((output_weight.T, keys, *query))
    near_weight = swap(weight, "yl")
    keys = keys.reshape(-1, depth)

    slot = lax.axis_index(DP) * slots + x_place
    places = jnp.stack([x_place, lengths[assignment[slot]]]).astype(jnp.int32)
    fresh = jnp.pad(new_latent, ((0, 0), (0, 16 - steps), (0, 0)))
    latent = pl.pallas_call(
        functools.partial(attend, steps, heads, width),
        out_shape=jax.ShapeDtypeStruct((slots, rows, width), jnp.bfloat16),
        in_specs=[SMEM] + [VMEM] * 6,
        out_specs=VMEM,
        compiler_params=pltpu.CompilerParams(vmem_limit_bytes=32 * 1024 * 1024),
        name="attend",
    )(places, *query, keys, fresh)

    latent = lax.all_to_all(latent, "x", split_axis=0, concat_axis=0, tiled=True)
    count = 1
    for axis in WIDE:
        count *= lax.axis_size(axis)
    n = slots * steps
    sent = pl.pallas_call(
        functools.partial(map_values, count, heads),
        out_shape=jax.ShapeDtypeStruct((count, 2 * n, heads // 2 * vhead), jnp.bfloat16),
        in_specs=[VMEM] * 3 + [pl.BlockSpec(memory_space=pl.ANY)],
        out_specs=VMEM,
        compiler_params=pltpu.CompilerParams(vmem_limit_bytes=32 * 1024 * 1024),
        name="map_values",
    )(latent, pick_rows(n, heads), value_weight, near_weight)

    sent = sent.reshape(count * 2 * n, heads // 2 * vhead)
    piece = lax.all_to_all(sent, WIDE, split_axis=0, concat_axis=0, tiled=True)
    weights = (weight, swap(weight, "core"), near_weight, swap(near_weight, "core"))
    own_columns = output_weight.shape[1] // groups
    blocks = jnp.stack([lax.axis_index("yl"), lax.axis_index("core")]).astype(jnp.int32)
    product = pl.pallas_call(
        project,
        out_shape=jax.ShapeDtypeStruct((4 * groups, own_columns, count * n), jnp.bfloat16),
        in_specs=[SMEM] + [VMEM] * 6,
        out_specs=VMEM,
        compiler_params=pltpu.CompilerParams(vmem_limit_bytes=32 * 1024 * 1024),
        name="project",
    )(blocks, piece, order_rows(count, n), *weights)
    terms = lax.all_to_all(product, BLOCKS + TENSOR, split_axis=0, concat_axis=0, tiled=True)
    terms = terms.reshape(4, groups, own_columns, -1)
    result = jnp.sum(terms.astype(jnp.float32), axis=1).astype(jnp.bfloat16)
    yh, yl, za, zb, core = (lax.axis_size(axis) for axis in DP)
    result = result.reshape(yl, core, own_columns, yh, za, zb, slots, steps)
    return result.transpose(3, 0, 4, 5, 1, 6, 7, 2).reshape(requests, steps, own_columns)


def solution(mesh):
    names = tuple(name for name, _ in SIZES)
    fine = Mesh(mesh.devices.reshape(tuple(size for _, size in SIZES)), names)
    return jax.shard_map(
        on_device,
        mesh=fine,
        in_specs=(
            P(None, DP + TENSOR, None),
            P(DP, None, TENSOR, None),
            P(DP, None, None),
            P(),
            P(),
            P(TENSOR, None, None),
            P(TENSOR, DP),
        ),
        out_specs=P(None, None, DP + TENSOR),
        check_vma=False,
    )
```

```python
import functools

import jax
import jax.numpy as jnp
from jax import lax
from jax.experimental import pallas as pl
from jax.experimental.pallas import tpu as pltpu
from jax.sharding import Mesh, PartitionSpec as P

score_scale = 192.0 ** (-0.5)
lowest = -1e30

DP = ("yh", "yl", "za", "zb", "core")
TENSOR = ("x", "zh")
SIZES = (("yh", 4), ("yl", 2), ("za", 2), ("zb", 2), ("core", 2), ("x", 4), ("zh", 2))
WIDE = ("yh", "za", "zb")
BLOCKS = ("yl", "core")

LIMIT = 16 * 1024 * 1024

VMEM = pl.BlockSpec(memory_space=pltpu.VMEM)
SMEM = pl.BlockSpec(memory_space=pltpu.SMEM)


def swap(array, axis):
    return lax.ppermute(array, axis, [(0, 1), (1, 0)])


def dot(a, b):
    return jnp.dot(a, b, preferred_element_type=jnp.float32)


def dot_rows(a, b):
    return lax.dot_general(a, b, (((1,), (1,)), ((), ())), preferred_element_type=jnp.float32)


def attend(steps, heads, width, place_ref, q0, q1, q2, q3, key_ref, fresh_ref, request_ref, out_ref):
    x, slot = place_ref[0], place_ref[2]
    lane = lax.broadcasted_iota(jnp.int32, (1, request_ref.shape[1]), 1)
    request = jnp.sum(jnp.where(lane == slot, request_ref[0:1], 0), axis=1, keepdims=True)
    limit = jnp.sum(jnp.where(lane == request, request_ref[1:2], 0), axis=1, keepdims=True)
    rows = steps * heads
    query = jnp.concatenate([q[...] for q in (q0, q1, q2, q3)], axis=0)
    fresh = fresh_ref[x]
    middle = key_ref.shape[0] // 2
    parts = [key_ref[:middle], key_ref[middle:]]
    scores = []
    for place, part in enumerate(parts):
        score = dot_rows(query, part) * score_scale
        index = lax.broadcasted_iota(jnp.int32, (1, score.shape[1]), 1)
        places = index // 8 * 16 + index % 8 // 2 * 4 + place * 2 + index % 2
        scores.append(jnp.where(places < limit, score, lowest))
    score = dot_rows(query, fresh) * score_scale
    row = lax.broadcasted_iota(jnp.int32, score.shape, 0)
    column = lax.broadcasted_iota(jnp.int32, score.shape, 1)
    scores.append(jnp.where(column <= (row % rows) // heads, score, lowest))
    top = functools.reduce(jnp.maximum, [jnp.max(score, axis=1, keepdims=True) for score in scores])
    total, summed = 0.0, 0.0
    for score, part in zip(scores, parts + [fresh]):
        raised = jnp.exp(score - top)
        total = total + jnp.sum(raised, axis=1, keepdims=True)
        summed = summed + dot(raised.astype(jnp.bfloat16), part[:, :width])
    latent = (summed / total).astype(jnp.bfloat16)
    for shift in range(4):
        out_ref[lax.rem(x + 4 - shift, 4)] = latent[shift * rows : (shift + 1) * rows]


def map_values(count, heads, latent_ref, value_ref, weight_ref, out_ref):
    latent = jnp.concatenate([latent_ref[slot] for slot in range(latent_ref.shape[0])], axis=0)
    n = latent.shape[0] // heads
    row = lax.broadcasted_iota(jnp.int32, (heads * 2 * n, 1), 0)
    head, line = row // (2 * n), row % (2 * n)
    source = jnp.where(line // n == head // (heads // 2), line % n * heads + head, -1)
    column = lax.broadcasted_iota(jnp.int32, (row.shape[0], latent.shape[0]), 1)
    pick = jnp.where(column == source, 1.0, 0.0).astype(jnp.bfloat16)
    picked = dot(pick, latent).astype(jnp.bfloat16)
    lines = out_ref.shape[1]
    half = heads // 2
    vhead = value_ref.shape[2]
    for h in range(half):
        value = dot(picked[h * lines : (h + 1) * lines], value_ref[h]) + dot(
            picked[(h + half) * lines : (h + half + 1) * lines], value_ref[h + half]
        )
        value = value.astype(jnp.bfloat16)
        for copy in range(count):
            out_ref[copy, :, h * vhead : (h + 1) * vhead] = value


def project(n, place_ref, piece_ref, own_ref, other_ref, out_ref):
    core, yl = place_ref[1], place_ref[3]
    every = piece_ref.shape[0]
    row = lax.broadcasted_iota(jnp.int32, (every, 1), 0)
    half, line = row // (every // 2), row % (every // 2)
    source = (line // n * 2 + half) * n + line % n
    column = lax.broadcasted_iota(jnp.int32, (every, every), 1)
    order = jnp.where(column == source, 1.0, 0.0).astype(jnp.bfloat16)
    lines = dot(order, piece_ref[...]).astype(jnp.bfloat16)
    rows, depth = lines.shape[0] // 2, lines.shape[1]
    groups = out_ref.shape[0] // 4
    columns = out_ref.shape[1]
    weight = jnp.concatenate([w[...] for w in (own_ref, other_ref)], axis=0)
    product = dot_rows(weight[:, :depth], lines[:rows]) + dot_rows(weight[:, depth:], lines[rows:])
    for block in range(4):
        other_y, other_core = block % 2, block // 2
        member = (1 - yl if other_y else yl) * 2 + (1 - core if other_core else core)
        for group in range(groups):
            start = (block * groups + group) * columns
            out_ref[member * groups + group] = product[start : start + columns].astype(jnp.bfloat16)


def on_device(cache, queries, new_latent, lengths, assignment, value_weight, output_weight):
    slots, steps, heads, depth = queries.shape
    requests, block = cache.shape[:2]
    width, vhead = value_weight.shape[1:]
    x_place, zh_count = lax.axis_index("x"), lax.axis_size("zh")
    groups = lax.axis_size("x") * zh_count
    rows = steps * heads

    order = (assignment[:, None] == jnp.arange(requests)[None, :]).astype(jnp.bfloat16)
    ordered = jnp.einsum(
        "jr,rpc->jpc", order, cache, preferred_element_type=jnp.float32
    ).astype(jnp.bfloat16)
    ordered = jnp.concatenate([ordered] * zh_count, axis=0)
    keys = lax.all_to_all(ordered, ("zh",) + DP + ("x",), split_axis=0, concat_axis=0, tiled=True)
    keys = keys.reshape(-1, depth)

    query = []
    for shift in range(4):
        both = lax.dynamic_index_in_dim(queries, lax.rem(x_place + shift, 4), 0, keepdims=False)
        both = both.reshape(rows, depth)
        if shift:
            both = lax.ppermute(both, "x", [(j, (j + shift) % 4) for j in range(4)])
        query.append(both)

    slot = lax.axis_index(DP) * slots + x_place
    places = jnp.stack([x_place, lax.axis_index("core"), slot, lax.axis_index("yl")]).astype(jnp.int32)
    limits = jnp.stack([assignment, lengths])
    fresh = jnp.pad(new_latent, ((0, 0), (0, 16 - steps), (0, 0)))
    weight, places, limits, fresh, keys, *query = lax.optimization_barrier(
        (output_weight.T, places, limits, fresh, keys, *query)
    )
    near_weight = swap(weight, "yl")
    latent = pl.pallas_call(
        functools.partial(attend, steps, heads, width),
        out_shape=jax.ShapeDtypeStruct((slots, rows, width), jnp.bfloat16),
        in_specs=[SMEM] + [VMEM] * 7,
        out_specs=VMEM,
        compiler_params=pltpu.CompilerParams(vmem_limit_bytes=LIMIT),
        name="attend",
    )(places, *query, keys, fresh, limits)

    latent = lax.all_to_all(latent, "x", split_axis=0, concat_axis=0, tiled=True)
    count = 1
    for axis in WIDE:
        count *= lax.axis_size(axis)
    n = slots * steps
    sent = pl.pallas_call(
        functools.partial(map_values, count, heads),
        out_shape=jax.ShapeDtypeStruct((count, 2 * n, heads // 2 * vhead), jnp.bfloat16),
        in_specs=[VMEM] * 3,
        out_specs=VMEM,
        compiler_params=pltpu.CompilerParams(vmem_limit_bytes=LIMIT),
        name="map_values",
    )(latent, value_weight, near_weight)

    sent = sent.reshape(count * 2 * n, heads // 2 * vhead)
    piece = lax.all_to_all(sent, WIDE, split_axis=0, concat_axis=0, tiled=True)
    weight = jnp.concatenate([weight, near_weight], axis=0)
    weights = (weight, swap(weight, "core"))
    own_columns = output_weight.shape[1] // groups
    product = pl.pallas_call(
        functools.partial(project, n),
        out_shape=jax.ShapeDtypeStruct((4 * groups, own_columns, count * n), jnp.bfloat16),
        in_specs=[SMEM] + [VMEM] * 3,
        out_specs=VMEM,
        compiler_params=pltpu.CompilerParams(vmem_limit_bytes=LIMIT),
        name="project",
    )(places, piece, *weights)
    terms = lax.all_to_all(product, BLOCKS + TENSOR, split_axis=0, concat_axis=0, tiled=True)
    terms = terms.reshape(4, groups, own_columns, -1)
    result = jnp.sum(terms.astype(jnp.float32), axis=1).astype(jnp.bfloat16)
    yh, yl, za, zb, core = (lax.axis_size(axis) for axis in DP)
    result = result.reshape(yl, core, own_columns, yh, za, zb, slots, steps)
    return result.transpose(3, 0, 4, 5, 1, 6, 7, 2).reshape(requests, steps, own_columns)


def solution(mesh):
    names = tuple(name for name, _ in SIZES)
    fine = Mesh(mesh.devices.reshape(tuple(size for _, size in SIZES)), names)
    return jax.shard_map(
        on_device,
        mesh=fine,
        in_specs=(
            P(None, DP + TENSOR, None),
            P(DP, None, TENSOR, None),
            P(DP, None, None),
            P(),
            P(),
            P(TENSOR, None, None),
            P(TENSOR, DP),
        ),
        out_specs=P(None, None, DP + TENSOR),
        check_vma=False,
    )
```

```python
import functools

import jax
import jax.numpy as jnp
from jax import lax
from jax.experimental import pallas as pl
from jax.experimental.pallas import tpu as pltpu
from jax.sharding import Mesh, PartitionSpec as P

score_scale = 192.0 ** (-0.5)
lowest = -1e30

DP = ("yh", "yl", "za", "zb", "core")
TENSOR = ("x", "zh")
SIZES = (("yh", 4), ("yl", 2), ("za", 2), ("zb", 2), ("core", 2), ("x", 4), ("zh", 2))
WIDE = ("yh", "za")
BLOCKS = ("yl", "zb", "core")

LIMIT = 16 * 1024 * 1024

VMEM = pl.BlockSpec(memory_space=pltpu.VMEM)
SMEM = pl.BlockSpec(memory_space=pltpu.SMEM)


def swap(array, axis):
    return lax.ppermute(array, axis, [(0, 1), (1, 0)])


def dot(a, b):
    return jnp.dot(a, b, preferred_element_type=jnp.float32)


def dot_rows(a, b):
    return lax.dot_general(a, b, (((1,), (1,)), ((), ())), preferred_element_type=jnp.float32)


def attend(steps, heads, width, place_ref, q0, q1, q2, q3, key_ref, fresh_ref, request_ref, out_ref):
    x, slot = place_ref[0], place_ref[2]
    lane = lax.broadcasted_iota(jnp.int32, (1, request_ref.shape[1]), 1)
    request = jnp.sum(jnp.where(lane == slot, request_ref[0:1], 0), axis=1, keepdims=True)
    limit = jnp.sum(jnp.where(lane == request, request_ref[1:2], 0), axis=1, keepdims=True)
    rows = steps * heads
    query = jnp.concatenate([q[...] for q in (q0, q1, q2, q3)], axis=0)
    fresh = fresh_ref[x]
    middle = key_ref.shape[0] // 2
    parts = [key_ref[:middle], key_ref[middle:]]
    scores = []
    for place, part in enumerate(parts):
        score = dot_rows(query, part) * score_scale
        index = lax.broadcasted_iota(jnp.int32, (1, score.shape[1]), 1)
        places = index // 8 * 16 + index % 8 // 2 * 4 + place * 2 + index % 2
        scores.append(jnp.where(places < limit, score, lowest))
    score = dot_rows(query, fresh) * score_scale
    row = lax.broadcasted_iota(jnp.int32, score.shape, 0)
    column = lax.broadcasted_iota(jnp.int32, score.shape, 1)
    scores.append(jnp.where(column <= (row % rows) // heads, score, lowest))
    top = functools.reduce(jnp.maximum, [jnp.max(score, axis=1, keepdims=True) for score in scores])
    total, summed = 0.0, 0.0
    for score, part in zip(scores, parts + [fresh]):
        raised = jnp.exp(score - top)
        total = total + jnp.sum(raised, axis=1, keepdims=True)
        summed = summed + dot(raised.astype(jnp.bfloat16), part[:, :width])
    latent = (summed / total).astype(jnp.bfloat16)
    for shift in range(4):
        out_ref[lax.rem(x + 4 - shift, 4)] = latent[shift * rows : (shift + 1) * rows]


def map_values(count, heads, latent_ref, value_ref, out_ref):
    latent = jnp.concatenate([latent_ref[slot] for slot in range(latent_ref.shape[0])], axis=0)
    n = latent.shape[0] // heads
    row = lax.broadcasted_iota(jnp.int32, (heads * 2 * n, 1), 0)
    head, line = row // (2 * n), row % (2 * n)
    source = jnp.where(line // n == head // (heads // 2), line % n * heads + head, -1)
    column = lax.broadcasted_iota(jnp.int32, (row.shape[0], latent.shape[0]), 1)
    pick = jnp.where(column == source, 1.0, 0.0).astype(jnp.bfloat16)
    picked = dot(pick, latent).astype(jnp.bfloat16)
    lines = out_ref.shape[1]
    half = heads // 2
    vhead = value_ref.shape[2]
    for h in range(half):
        value = dot(picked[h * lines : (h + 1) * lines], value_ref[h]) + dot(
            picked[(h + half) * lines : (h + half + 1) * lines], value_ref[h + half]
        )
        value = value.astype(jnp.bfloat16)
        for copy in range(count):
            out_ref[copy, :, h * vhead : (h + 1) * vhead] = value


def project(n, place_ref, piece_ref, own_ref, other_ref, out_ref):
    core, yl, zb = place_ref[1], place_ref[3], place_ref[4]
    every = piece_ref.shape[0]
    row = lax.broadcasted_iota(jnp.int32, (every, 1), 0)
    half, line = row // (every // 2), row % (every // 2)
    source = (line // n * 2 + half) * n + line % n
    column = lax.broadcasted_iota(jnp.int32, (every, every), 1)
    order = jnp.where(column == source, 1.0, 0.0).astype(jnp.bfloat16)
    lines = dot(order, piece_ref[...]).astype(jnp.bfloat16)
    rows, depth = lines.shape[0] // 2, lines.shape[1]
    groups = out_ref.shape[0] // 8
    columns = out_ref.shape[1]
    weight = jnp.concatenate([w[...] for w in (own_ref, other_ref)], axis=0)
    product = dot_rows(weight[:, :depth], lines[:rows]) + dot_rows(weight[:, depth:], lines[rows:])
    for block in range(8):
        other_core, other_y, other_z = block // 4, block // 2 % 2, block % 2
        member = (1 - yl if other_y else yl) * 2 + (1 - zb if other_z else zb)
        member = member * 2 + (1 - core if other_core else core)
        for group in range(groups):
            start = (block * groups + group) * columns
            out_ref[member * groups + group] = product[start : start + columns].astype(jnp.bfloat16)


def on_device(cache, queries, new_latent, lengths, assignment, value_weight, output_weight):
    slots, steps, heads, depth = queries.shape
    requests, block = cache.shape[:2]
    width, vhead = value_weight.shape[1:]
    x_place, zh_count = lax.axis_index("x"), lax.axis_size("zh")
    groups = lax.axis_size("x") * zh_count
    rows = steps * heads

    order = (assignment[:, None] == jnp.arange(requests)[None, :]).astype(jnp.bfloat16)
    ordered = jnp.einsum(
        "jr,rpc->jpc", order, cache, preferred_element_type=jnp.float32
    ).astype(jnp.bfloat16)
    ordered = jnp.concatenate([ordered] * zh_count, axis=0)
    keys = lax.all_to_all(ordered, ("zh",) + DP + ("x",), split_axis=0, concat_axis=0, tiled=True)
    keys = keys.reshape(-1, depth)

    query = []
    for shift in range(4):
        both = lax.dynamic_index_in_dim(queries, lax.rem(x_place + shift, 4), 0, keepdims=False)
        both = both.reshape(rows, depth)
        if shift:
            both = lax.ppermute(both, "x", [(j, (j + shift) % 4) for j in range(4)])
        query.append(both)

    slot = lax.axis_index(DP) * slots + x_place
    places = jnp.stack([x_place, lax.axis_index("core"), slot, lax.axis_index("yl"), lax.axis_index("zb")]).astype(jnp.int32)
    limits = jnp.stack([assignment, lengths])
    fresh = jnp.pad(new_latent, ((0, 0), (0, 16 - steps), (0, 0)))
    weight, places, limits, fresh, *query = lax.optimization_barrier(
        (output_weight.T, places, limits, fresh, *query)
    )
    near_weights = [
        lax.ppermute(weight, ("yl", "zb"), [(j, j ^ step) for j in range(4)]) for step in (1, 2, 3)
    ]
    latent = pl.pallas_call(
        functools.partial(attend, steps, heads, width),
        out_shape=jax.ShapeDtypeStruct((slots, rows, width), jnp.bfloat16),
        in_specs=[SMEM] + [VMEM] * 7,
        out_specs=VMEM,
        compiler_params=pltpu.CompilerParams(vmem_limit_bytes=LIMIT),
        name="attend",
    )(places, *query, keys, fresh, limits)

    latent = lax.all_to_all(latent, "x", split_axis=0, concat_axis=0, tiled=True)
    count = 1
    for axis in WIDE:
        count *= lax.axis_size(axis)
    n = slots * steps
    sent = pl.pallas_call(
        functools.partial(map_values, count, heads),
        out_shape=jax.ShapeDtypeStruct((count, 2 * n, heads // 2 * vhead), jnp.bfloat16),
        in_specs=[VMEM] * 2,
        out_specs=VMEM,
        compiler_params=pltpu.CompilerParams(vmem_limit_bytes=LIMIT),
        name="map_values",
    )(latent, value_weight)

    sent = sent.reshape(count * 2 * n, heads // 2 * vhead)
    sent, *near_weights = lax.optimization_barrier((sent, *near_weights))
    piece = lax.all_to_all(sent, WIDE, split_axis=0, concat_axis=0, tiled=True)
    weight = jnp.concatenate([weight, *near_weights], axis=0)
    weights = (weight, swap(weight, "core"))
    own_columns = output_weight.shape[1] // groups
    product = pl.pallas_call(
        functools.partial(project, n),
        out_shape=jax.ShapeDtypeStruct((8 * groups, own_columns, count * n), jnp.bfloat16),
        in_specs=[SMEM] + [VMEM] * 3,
        out_specs=VMEM,
        compiler_params=pltpu.CompilerParams(vmem_limit_bytes=LIMIT),
        name="project",
    )(places, piece, *weights)
    terms = lax.all_to_all(product, BLOCKS + TENSOR, split_axis=0, concat_axis=0, tiled=True)
    terms = terms.reshape(8, groups, own_columns, -1)
    result = jnp.sum(terms.astype(jnp.float32), axis=1).astype(jnp.bfloat16)
    yh, yl, za, zb, core = (lax.axis_size(axis) for axis in DP)
    result = result.reshape(yl, zb, core, own_columns, yh, za, slots, steps)
    return result.transpose(4, 0, 5, 1, 2, 6, 7, 3).reshape(requests, steps, own_columns)


def solution(mesh):
    names = tuple(name for name, _ in SIZES)
    fine = Mesh(mesh.devices.reshape(tuple(size for _, size in SIZES)), names)
    return jax.shard_map(
        on_device,
        mesh=fine,
        in_specs=(
            P(None, DP + TENSOR, None),
            P(DP, None, TENSOR, None),
            P(DP, None, None),
            P(),
            P(),
            P(TENSOR, None, None),
            P(TENSOR, DP),
        ),
        out_specs=P(None, None, DP + TENSOR),
        check_vma=False,
    )
```

```python
import functools

import jax
import jax.numpy as jnp
from jax import lax
from jax.experimental import pallas as pl
from jax.experimental.pallas import tpu as pltpu
from jax.sharding import Mesh, PartitionSpec as P

score_scale = 192.0 ** (-0.5)
lowest = -1e30

DP = ("yh", "yl", "za", "zb", "core")
TENSOR = ("x", "zh")
SIZES = (("yh", 4), ("yl", 2), ("za", 2), ("zb", 2), ("core", 2), ("x", 4), ("zh", 2))
WIDE = ("yh", "za")
BLOCKS = ("yl", "zb", "core")

LIMIT = 16 * 1024 * 1024

VMEM = pl.BlockSpec(memory_space=pltpu.VMEM)
SMEM = pl.BlockSpec(memory_space=pltpu.SMEM)


def swap(array, axis):
    return lax.ppermute(array, axis, [(0, 1), (1, 0)])


def dot(a, b):
    return jnp.dot(a, b, preferred_element_type=jnp.float32)


def dot_rows(a, b):
    return lax.dot_general(a, b, (((1,), (1,)), ((), ())), preferred_element_type=jnp.float32)


def attend(steps, heads, width, place_ref, q0, q1, q2, q3, key_ref, fresh_ref, request_ref, value_ref, out_ref):
    x, slot = place_ref[0], place_ref[2]
    lane = lax.broadcasted_iota(jnp.int32, (1, request_ref.shape[1]), 1)
    request = jnp.sum(jnp.where(lane == slot, request_ref[0:1], 0), axis=1, keepdims=True)
    limit = jnp.sum(jnp.where(lane == request, request_ref[1:2], 0), axis=1, keepdims=True)
    rows = steps * heads
    query = jnp.concatenate([q[...] for q in (q0, q1, q2, q3)], axis=0)
    fresh = fresh_ref[x]
    middle = key_ref.shape[0] // 2
    parts = [key_ref[:middle], key_ref[middle:]]
    scores = []
    for place, part in enumerate(parts):
        score = dot_rows(query, part) * score_scale
        index = lax.broadcasted_iota(jnp.int32, (1, score.shape[1]), 1)
        places = index // 8 * 16 + index % 8 // 2 * 4 + place * 2 + index % 2
        scores.append(jnp.where(places < limit, score, lowest))
    score = dot_rows(query, fresh) * score_scale
    row = lax.broadcasted_iota(jnp.int32, score.shape, 0)
    column = lax.broadcasted_iota(jnp.int32, score.shape, 1)
    scores.append(jnp.where(column <= (row % rows) // heads, score, lowest))
    top = functools.reduce(jnp.maximum, [jnp.max(score, axis=1, keepdims=True) for score in scores])
    total, summed = 0.0, 0.0
    for score, part in zip(scores, parts + [fresh]):
        raised = jnp.exp(score - top)
        total = total + jnp.sum(raised, axis=1, keepdims=True)
        summed = summed + dot(raised.astype(jnp.bfloat16), part[:, :width])
    latent = (summed / total).astype(jnp.bfloat16)
    for shift in range(4):
        out_ref[lax.rem(x + 4 - shift, 4)] = latent[shift * rows : (shift + 1) * rows]


def map_values(count, heads, latent_ref, value_ref, out_ref):
    latent = jnp.concatenate([latent_ref[slot] for slot in range(latent_ref.shape[0])], axis=0)
    n = latent.shape[0] // heads
    row = lax.broadcasted_iota(jnp.int32, (heads * 2 * n, 1), 0)
    head, line = row // (2 * n), row % (2 * n)
    source = jnp.where(line // n == head // (heads // 2), line % n * heads + head, -1)
    column = lax.broadcasted_iota(jnp.int32, (row.shape[0], latent.shape[0]), 1)
    pick = jnp.where(column == source, 1.0, 0.0).astype(jnp.bfloat16)
    picked = dot(pick, latent).astype(jnp.bfloat16)
    lines = out_ref.shape[1]
    half = heads // 2
    vhead = value_ref.shape[2]
    for h in range(half):
        value = dot(picked[h * lines : (h + 1) * lines], value_ref[h]) + dot(
            picked[(h + half) * lines : (h + half + 1) * lines], value_ref[h + half]
        )
        value = value.astype(jnp.bfloat16)
        for copy in range(count):
            out_ref[copy, :, h * vhead : (h + 1) * vhead] = value


def project(n, place_ref, piece_ref, *refs):
    *weight_refs, out_ref = refs
    core, yl, zb = place_ref[1], place_ref[3], place_ref[4]
    every = piece_ref.shape[0]
    row = lax.broadcasted_iota(jnp.int32, (every, 1), 0)
    half, line = row // (every // 2), row % (every // 2)
    source = (line // n * 2 + half) * n + line % n
    column = lax.broadcasted_iota(jnp.int32, (every, every), 1)
    order = jnp.where(column == source, 1.0, 0.0).astype(jnp.bfloat16)
    lines = dot(order, piece_ref[...]).astype(jnp.bfloat16)
    rows, depth = lines.shape[0] // 2, lines.shape[1]
    groups = out_ref.shape[0] // 8
    columns = out_ref.shape[1]
    weight = jnp.concatenate([w[...] for w in weight_refs], axis=0)
    product = dot_rows(weight[:, :depth], lines[:rows]) + dot_rows(weight[:, depth:], lines[rows:])
    for block in range(8):
        other_core, other_y, other_z = block // 4, block // 2 % 2, block % 2
        member = (1 - yl if other_y else yl) * 2 + (1 - zb if other_z else zb)
        member = member * 2 + (1 - core if other_core else core)
        for group in range(groups):
            start = (block * groups + group) * columns
            out_ref[member * groups + group] = product[start : start + columns].astype(jnp.bfloat16)


def on_device(cache, queries, new_latent, lengths, assignment, value_weight, output_weight):
    slots, steps, heads, depth = queries.shape
    requests, block = cache.shape[:2]
    width, vhead = value_weight.shape[1:]
    x_place, zh_count = lax.axis_index("x"), lax.axis_size("zh")
    groups = lax.axis_size("x") * zh_count
    rows = steps * heads

    order = (assignment[:, None] == jnp.arange(requests)[None, :]).astype(jnp.bfloat16)
    ordered = jnp.einsum(
        "jr,rpc->jpc", order, cache, preferred_element_type=jnp.float32
    ).astype(jnp.bfloat16)
    ordered = jnp.concatenate([ordered] * zh_count, axis=0)
    keys = lax.all_to_all(ordered, ("zh",) + DP + ("x",), split_axis=0, concat_axis=0, tiled=True)
    keys = keys.reshape(-1, depth)

    query = []
    for shift in range(4):
        both = lax.dynamic_index_in_dim(queries, lax.rem(x_place + shift, 4), 0, keepdims=False)
        both = both.reshape(rows, depth)
        if shift:
            both = lax.ppermute(both, "x", [(j, (j + shift) % 4) for j in range(4)])
        query.append(both)

    slot = lax.axis_index(DP) * slots + x_place
    places = jnp.stack([x_place, lax.axis_index("core"), slot, lax.axis_index("yl"), lax.axis_index("zb")]).astype(jnp.int32)
    limits = jnp.stack([assignment, lengths])
    fresh = jnp.pad(new_latent, ((0, 0), (0, 16 - steps), (0, 0)))
    weight, places, limits, fresh, *query = lax.optimization_barrier(
        (output_weight.T, places, limits, fresh, *query)
    )
    near_weights = [
        lax.ppermute(weight, ("yl", "zb"), [(j, j ^ step) for j in range(4)]) for step in (1, 2, 3)
    ]
    latent = pl.pallas_call(
        functools.partial(attend, steps, heads, width),
        out_shape=jax.ShapeDtypeStruct((slots, rows, width), jnp.bfloat16),
        in_specs=[SMEM] + [VMEM] * 8,
        out_specs=VMEM,
        compiler_params=pltpu.CompilerParams(vmem_limit_bytes=LIMIT),
        name="attend",
    )(places, *query, keys, fresh, limits, value_weight)

    latent = lax.all_to_all(latent, "x", split_axis=0, concat_axis=0, tiled=True)
    count = 1
    for axis in WIDE:
        count *= lax.axis_size(axis)
    n = slots * steps
    sent = pl.pallas_call(
        functools.partial(map_values, count, heads),
        out_shape=jax.ShapeDtypeStruct((count, 2 * n, heads // 2 * vhead), jnp.bfloat16),
        in_specs=[VMEM] * 2,
        out_specs=VMEM,
        compiler_params=pltpu.CompilerParams(vmem_limit_bytes=LIMIT),
        name="map_values",
    )(latent, value_weight)

    sent = sent.reshape(count * 2 * n, heads // 2 * vhead)
    sent, *near_weights = lax.optimization_barrier((sent, *near_weights))
    piece = lax.all_to_all(sent, WIDE, split_axis=0, concat_axis=0, tiled=True)
    weights = [weight, *near_weights]
    weights += [swap(part, "core") for part in weights]
    own_columns = output_weight.shape[1] // groups
    product = pl.pallas_call(
        functools.partial(project, n),
        out_shape=jax.ShapeDtypeStruct((8 * groups, own_columns, count * n), jnp.bfloat16),
        in_specs=[SMEM] + [VMEM] * 9,
        out_specs=VMEM,
        compiler_params=pltpu.CompilerParams(vmem_limit_bytes=LIMIT),
        name="project",
    )(places, piece, *weights)
    terms = lax.all_to_all(product, BLOCKS + TENSOR, split_axis=0, concat_axis=0, tiled=True)
    terms = terms.reshape(8, groups, own_columns, -1)
    result = jnp.sum(terms.astype(jnp.float32), axis=1).astype(jnp.bfloat16)
    yh, yl, za, zb, core = (lax.axis_size(axis) for axis in DP)
    result = result.reshape(yl, zb, core, own_columns, yh, za, slots, steps)
    return result.transpose(4, 0, 5, 1, 2, 6, 7, 3).reshape(requests, steps, own_columns)


def solution(mesh):
    names = tuple(name for name, _ in SIZES)
    fine = Mesh(mesh.devices.reshape(tuple(size for _, size in SIZES)), names)
    return jax.shard_map(
        on_device,
        mesh=fine,
        in_specs=(
            P(None, DP + TENSOR, None),
            P(DP, None, TENSOR, None),
            P(DP, None, None),
            P(),
            P(),
            P(TENSOR, None, None),
            P(TENSOR, DP),
        ),
        out_specs=P(None, None, DP + TENSOR),
        check_vma=False,
    )
```

```python
import functools

import jax
import jax.numpy as jnp
from jax import lax
from jax.experimental import pallas as pl
from jax.experimental.pallas import tpu as pltpu
from jax.sharding import Mesh, PartitionSpec as P

score_scale = 192.0 ** (-0.5)
lowest = -1e30

DP = ("yh", "yl", "za", "zb", "core")
TENSOR = ("x", "zh")
SIZES = (("yh", 4), ("yl", 2), ("za", 2), ("zb", 2), ("core", 2), ("x", 4), ("zh", 2))
WIDE = ("yh", "za")
BLOCKS = ("yl", "zb", "core")

LIMIT = 16 * 1024 * 1024

VMEM = pl.BlockSpec(memory_space=pltpu.VMEM)
SMEM = pl.BlockSpec(memory_space=pltpu.SMEM)


def swap(array, axis):
    return lax.ppermute(array, axis, [(0, 1), (1, 0)])


def dot(a, b):
    return jnp.dot(a, b, preferred_element_type=jnp.float32)


def dot_rows(a, b):
    return lax.dot_general(a, b, (((1,), (1,)), ((), ())), preferred_element_type=jnp.float32)


def attend(steps, heads, width, place_ref, q0, q1, q2, q3, key_ref, fresh_ref, request_ref, value_ref, weight_ref, out_ref):
    x, slot = place_ref[0], place_ref[2]
    lane = lax.broadcasted_iota(jnp.int32, (1, request_ref.shape[1]), 1)
    request = jnp.sum(jnp.where(lane == slot, request_ref[0:1], 0), axis=1, keepdims=True)
    limit = jnp.sum(jnp.where(lane == request, request_ref[1:2], 0), axis=1, keepdims=True)
    rows = steps * heads
    query = jnp.concatenate([q[...] for q in (q0, q1, q2, q3)], axis=0)
    fresh = fresh_ref[x]
    middle = key_ref.shape[0] // 2
    parts = [key_ref[:middle], key_ref[middle:]]
    scores = []
    for place, part in enumerate(parts):
        score = dot_rows(query, part) * score_scale
        index = lax.broadcasted_iota(jnp.int32, (1, score.shape[1]), 1)
        places = index // 8 * 16 + index % 8 // 2 * 4 + place * 2 + index % 2
        scores.append(jnp.where(places < limit, score, lowest))
    score = dot_rows(query, fresh) * score_scale
    row = lax.broadcasted_iota(jnp.int32, score.shape, 0)
    column = lax.broadcasted_iota(jnp.int32, score.shape, 1)
    scores.append(jnp.where(column <= (row % rows) // heads, score, lowest))
    top = functools.reduce(jnp.maximum, [jnp.max(score, axis=1, keepdims=True) for score in scores])
    total, summed = 0.0, 0.0
    for score, part in zip(scores, parts + [fresh]):
        raised = jnp.exp(score - top)
        total = total + jnp.sum(raised, axis=1, keepdims=True)
        summed = summed + dot(raised.astype(jnp.bfloat16), part[:, :width])
    latent = (summed / total).astype(jnp.bfloat16)
    for shift in range(4):
        out_ref[lax.rem(x + 4 - shift, 4)] = latent[shift * rows : (shift + 1) * rows]


def map_values(count, heads, latent_ref, value_ref, out_ref):
    latent = jnp.concatenate([latent_ref[slot] for slot in range(latent_ref.shape[0])], axis=0)
    n = latent.shape[0] // heads
    row = lax.broadcasted_iota(jnp.int32, (heads * 2 * n, 1), 0)
    head, line = row // (2 * n), row % (2 * n)
    source = jnp.where(line // n == head // (heads // 2), line % n * heads + head, -1)
    column = lax.broadcasted_iota(jnp.int32, (row.shape[0], latent.shape[0]), 1)
    pick = jnp.where(column == source, 1.0, 0.0).astype(jnp.bfloat16)
    picked = dot(pick, latent).astype(jnp.bfloat16)
    lines = out_ref.shape[1]
    half = heads // 2
    vhead = value_ref.shape[2]
    for h in range(half):
        value = dot(picked[h * lines : (h + 1) * lines], value_ref[h]) + dot(
            picked[(h + half) * lines : (h + half + 1) * lines], value_ref[h + half]
        )
        value = value.astype(jnp.bfloat16)
        for copy in range(count):
            out_ref[copy, :, h * vhead : (h + 1) * vhead] = value


def project(n, place_ref, piece_ref, *refs):
    *weight_refs, out_ref = refs
    core, yl, zb = place_ref[1], place_ref[3], place_ref[4]
    every = piece_ref.shape[0]
    row = lax.broadcasted_iota(jnp.int32, (every, 1), 0)
    half, line = row // (every // 2), row % (every // 2)
    source = (line // n * 2 + half) * n + line % n
    column = lax.broadcasted_iota(jnp.int32, (every, every), 1)
    order = jnp.where(column == source, 1.0, 0.0).astype(jnp.bfloat16)
    lines = dot(order, piece_ref[...]).astype(jnp.bfloat16)
    rows, depth = lines.shape[0] // 2, lines.shape[1]
    groups = out_ref.shape[0] // 8
    columns = out_ref.shape[1]
    weight = jnp.concatenate([w[...] for w in weight_refs], axis=0)
    product = dot_rows(weight[:, :depth], lines[:rows]) + dot_rows(weight[:, depth:], lines[rows:])
    for block in range(8):
        other_core, other_y, other_z = block // 4, block // 2 % 2, block % 2
        member = (1 - yl if other_y else yl) * 2 + (1 - zb if other_z else zb)
        member = member * 2 + (1 - core if other_core else core)
        for group in range(groups):
            start = (block * groups + group) * columns
            out_ref[member * groups + group] = product[start : start + columns].astype(jnp.bfloat16)


def on_device(cache, queries, new_latent, lengths, assignment, value_weight, output_weight):
    slots, steps, heads, depth = queries.shape
    requests, block = cache.shape[:2]
    width, vhead = value_weight.shape[1:]
    x_place, zh_count = lax.axis_index("x"), lax.axis_size("zh")
    groups = lax.axis_size("x") * zh_count
    rows = steps * heads

    order = (assignment[:, None] == jnp.arange(requests)[None, :]).astype(jnp.bfloat16)
    ordered = jnp.einsum(
        "jr,rpc->jpc", order, cache, preferred_element_type=jnp.float32
    ).astype(jnp.bfloat16)
    ordered = jnp.concatenate([ordered] * zh_count, axis=0)
    keys = lax.all_to_all(ordered, ("zh",) + DP + ("x",), split_axis=0, concat_axis=0, tiled=True)
    keys = keys.reshape(-1, depth)

    query = []
    for shift in range(4):
        both = lax.dynamic_index_in_dim(queries, lax.rem(x_place + shift, 4), 0, keepdims=False)
        both = both.reshape(rows, depth)
        if shift:
            both = lax.ppermute(both, "x", [(j, (j + shift) % 4) for j in range(4)])
        query.append(both)

    slot = lax.axis_index(DP) * slots + x_place
    places = jnp.stack([x_place, lax.axis_index("core"), slot, lax.axis_index("yl"), lax.axis_index("zb")]).astype(jnp.int32)
    limits = jnp.stack([assignment, lengths])
    fresh = jnp.pad(new_latent, ((0, 0), (0, 16 - steps), (0, 0)))
    weight, places, limits, fresh, *query = lax.optimization_barrier(
        (output_weight.T, places, limits, fresh, *query)
    )
    other_weight = swap(weight, "core")
    near_weights = [
        lax.ppermute(weight, ("yl", "zb"), [(j, j ^ step) for j in range(4)]) for step in (1, 2, 3)
    ]
    latent = pl.pallas_call(
        functools.partial(attend, steps, heads, width),
        out_shape=jax.ShapeDtypeStruct((slots, rows, width), jnp.bfloat16),
        in_specs=[SMEM] + [VMEM] * 9,
        out_specs=VMEM,
        compiler_params=pltpu.CompilerParams(vmem_limit_bytes=LIMIT),
        name="attend",
    )(places, *query, keys, fresh, limits, value_weight, other_weight)

    latent = lax.all_to_all(latent, "x", split_axis=0, concat_axis=0, tiled=True)
    count = 1
    for axis in WIDE:
        count *= lax.axis_size(axis)
    n = slots * steps
    sent = pl.pallas_call(
        functools.partial(map_values, count, heads),
        out_shape=jax.ShapeDtypeStruct((count, 2 * n, heads // 2 * vhead), jnp.bfloat16),
        in_specs=[VMEM] * 2,
        out_specs=VMEM,
        compiler_params=pltpu.CompilerParams(vmem_limit_bytes=LIMIT),
        name="map_values",
    )(latent, value_weight)

    sent = sent.reshape(count * 2 * n, heads // 2 * vhead)
    sent, *near_weights = lax.optimization_barrier((sent, *near_weights))
    piece = lax.all_to_all(sent, WIDE, split_axis=0, concat_axis=0, tiled=True)
    weights = [weight, *near_weights, other_weight] + [swap(part, "core") for part in near_weights]
    own_columns = output_weight.shape[1] // groups
    product = pl.pallas_call(
        functools.partial(project, n),
        out_shape=jax.ShapeDtypeStruct((8 * groups, own_columns, count * n), jnp.bfloat16),
        in_specs=[SMEM] + [VMEM] * 9,
        out_specs=VMEM,
        compiler_params=pltpu.CompilerParams(vmem_limit_bytes=LIMIT),
        name="project",
    )(places, piece, *weights)
    terms = lax.all_to_all(product, BLOCKS + TENSOR, split_axis=0, concat_axis=0, tiled=True)
    terms = terms.reshape(8, groups, own_columns, -1)
    result = jnp.sum(terms.astype(jnp.float32), axis=1).astype(jnp.bfloat16)
    yh, yl, za, zb, core = (lax.axis_size(axis) for axis in DP)
    result = result.reshape(yl, zb, core, own_columns, yh, za, slots, steps)
    return result.transpose(4, 0, 5, 1, 2, 6, 7, 3).reshape(requests, steps, own_columns)


def solution(mesh):
    names = tuple(name for name, _ in SIZES)
    fine = Mesh(mesh.devices.reshape(tuple(size for _, size in SIZES)), names)
    return jax.shard_map(
        on_device,
        mesh=fine,
        in_specs=(
            P(None, DP + TENSOR, None),
            P(DP, None, TENSOR, None),
            P(DP, None, None),
            P(),
            P(),
            P(TENSOR, None, None),
            P(TENSOR, DP),
        ),
        out_specs=P(None, None, DP + TENSOR),
        check_vma=False,
    )
```
